512 devices in a mesh: blk: 512 (over z, y, x, core).
Axes of the slice: x: 4, y: 4, z: 16, core: 2. Of those that a mesh axis runs over, the one named last changes fastest.
Arguments:
- picture_vectors: float32 [131072, 1152], P('blk'), may hold values from -1.5909903 to 1.5909903
- caption_vectors: float32 [131072, 1152], P('blk'), may hold values from -2.2391715 to 2.2391715
- sharpness_factor: float32 [1], replicated, may hold values from 6 to 14
- additive_shift_term: float32 [1], replicated, may hold values from -7 to -4
Outputs:
- loss_rows: float32 [131072], P('blk')
- grad_image: float32 [131072, 1152], P('blk')
- text_gradient: float32 [131072, 1152], P('blk')
The draws below stay inside these ranges and needn't reach their ends.
All inputs are finite; a program needn't handle non-finite values.
Results may differ from the reference program's by a relative error of at most 0.0003.
Values sent between devices are 32-bit elements; how exact they have to be, the bound alone decides.
No kernel may reach another device: no remote copies, remote signals or barrier semaphores. Data moves between devices by JAX's collectives and lax.ppermute only.
A program may use at most 64 MiB of HBM per device.

```python
import math
import jax
import jax.numpy as jnp
from jax import lax

D = 1152
TOK_DEV = 256
HOPS = 4
PAIR_COUNT = 131072


def common_parts(key):
    column_key = jax.random.fold_in(key, 100)
    shared_key = jax.random.fold_in(key, 101)
    matrix_fields = jnp.exp(jax.random.uniform(column_key, (D,), jnp.float32, jnp.log(0.1), jnp.log(3.0)))
    shared = jnp.clip(jax.random.normal(shared_key, (PAIR_COUNT, D), jnp.float32), -6.0, 6.0)
    return (matrix_fields, shared)


def row_scales(key, lower, upper):
    return jnp.exp(jax.random.uniform(key, (PAIR_COUNT, 1), jnp.float32, jnp.log(lower), jnp.log(upper)))


def draw_picture_vectors(key, part):
    matrix_fields, shared = common_parts(key)
    key = jax.random.fold_in(key, 1)
    rows = row_scales(key, 0.3, 3.0)
    return shared * matrix_fields * rows * D ** (-0.5)


def draw_caption_vectors(key, part):
    matrix_fields, shared = common_parts(key)
    key = jax.random.fold_in(key, 2)
    noise_key = jax.random.fold_in(key, 3)
    rows = row_scales(key, 0.3, 3.0)
    noise = jnp.clip(jax.random.normal(noise_key, (PAIR_COUNT, D), jnp.float32), -6.0, 6.0)
    return (0.6 * shared + 0.8 * noise) * matrix_fields * rows * D ** (-0.5)


def setup_inputs(seed: int = 0) -> dict:
    key_list = jax.random.split(jax.random.key(seed), 5)
    picture_vectors = draw_picture_vectors(jax.random.fold_in(key_list[4], 71), 0)
    caption_vectors = draw_caption_vectors(jax.random.fold_in(key_list[4], 71), 0)
    sharpness_factor = jnp.clip(jnp.exp(jax.random.uniform(key_list[2], (1,), jnp.float32, math.log(6.0), math.log(14.0))), 6.0, 14.0)
    additive_shift_term = jnp.clip(jax.random.uniform(key_list[3], (1,), jnp.float32, -7.0, -4.0), -7.0, -4.0)
    return {"picture_vectors": picture_vectors, "caption_vectors": caption_vectors, "sharpness_factor": sharpness_factor, "additive_shift_term": additive_shift_term}


EPS = 1e-06
HIGH = lax.Precision.HIGHEST

def normalize(raw):
    inverse_norm = lax.rsqrt(lax.optimization_barrier(jnp.sum(raw * raw, axis=-1, keepdims=True)) + EPS)
    return (raw * inverse_norm, inverse_norm)

def restore(raw, inverse_norm, grad):
    inner = lax.optimization_barrier(jnp.sum(raw * grad, axis=-1, keepdims=True))
    return inverse_norm * grad - inverse_norm * inverse_norm * inverse_norm * inner * raw

def reference(picture_vectors, caption_vectors, sharpness_factor, additive_shift_term):
    block_count = PAIR_COUNT // TOK_DEV
    image_unit, inv_image = normalize(picture_vectors)
    caption_direction, inv_text = normalize(caption_vectors)
    left = image_unit.reshape(block_count, TOK_DEV, D)
    right = caption_direction.reshape(block_count, TOK_DEV, D)
    similarity_multiplier = sharpness_factor[0]
    block_offset = additive_shift_term[0]
    loss = jnp.zeros((block_count, TOK_DEV), jnp.float32)
    grad_left = jnp.zeros((block_count, TOK_DEV, D), jnp.float32)
    grad_right = jnp.zeros((block_count, TOK_DEV, D), jnp.float32)
    for step in range(HOPS):
        partner = jnp.roll(right, step, axis=0)
        if step == 0:
            positive = jnp.eye(TOK_DEV, dtype=jnp.float32)
        else:
            positive = jnp.zeros((TOK_DEV, TOK_DEV), jnp.float32)
        logits = jnp.einsum('nad,nbd->nab', left, partner, precision=HIGH)
        rolled_text = similarity_multiplier * logits + block_offset
        terms = jax.nn.softplus(rolled_text - 2.0 * positive * rolled_text)
        weight = similarity_multiplier * (jax.nn.sigmoid(rolled_text) - positive)
        loss = loss + lax.optimization_barrier(jnp.sum(terms, axis=-1))
        grad_left = grad_left + jnp.einsum('nab,nbd->nad', weight, partner, precision=HIGH)
        share = jnp.einsum('nab,nad->nbd', weight, left, precision=HIGH)
        grad_right = grad_right + jnp.roll(share, -step, axis=0)
    loss_rows = (loss / HOPS).reshape(PAIR_COUNT)
    grad_image = restore(picture_vectors, inv_image, grad_left.reshape(PAIR_COUNT, D))
    text_gradient = restore(caption_vectors, inv_text, grad_right.reshape(PAIR_COUNT, D))
    return (loss_rows, grad_image, text_gradient)
```

```python
import jax
import jax.numpy as jnp
from jax import lax
from jax.sharding import PartitionSpec as P

HOPS = 4
EPS = 1e-06
HIGH = lax.Precision.HIGH


def across(value):
    count = lax.axis_size("blk")
    pairs = [(i, (i + 1 if i % 2 else i - 1) % count) for i in range(count)]
    return lax.ppermute(value, "blk", pairs)


def in_chip(value):
    count = lax.axis_size("blk")
    return lax.ppermute(value, "blk", [(i, i ^ 1) for i in range(count)])


def normalize(raw):
    inverse_norm = lax.rsqrt(jnp.sum(raw * raw, axis=-1, keepdims=True) + EPS)
    return (raw * inverse_norm, inverse_norm)


def restore(raw, inverse_norm, grad):
    inner = jnp.sum(raw * grad, axis=-1, keepdims=True)
    return inverse_norm * grad - inverse_norm * inverse_norm * inverse_norm * inner * raw


def dot(a, b, ca, cb):
    return lax.dot_general(
        a, b, (((ca,), (cb,)), ((), ())), precision=HIGH, preferred_element_type=jnp.float32
    )


def body(picture_vectors, caption_vectors, sharpness_factor, additive_shift_term):
    rows = picture_vectors.shape[0]
    scale = sharpness_factor[0]
    shift = additive_shift_term[0]
    even = lax.axis_index("blk") % 2 == 0

    def pair(a, b, positive=None):
        shifted = scale * dot(a, b, 1, 1) + shift
        if positive is None:
            return jax.nn.softplus(shifted), scale * jax.nn.sigmoid(shifted)
        terms = jax.nn.softplus(shifted - 2.0 * positive * shifted)
        return terms, scale * (jax.nn.sigmoid(shifted) - positive)

    p_raw = jnp.where(even, picture_vectors, caption_vectors)
    q_raw = jnp.where(even, caption_vectors, picture_vectors)
    p, inv_p = normalize(p_raw)
    q, inv_q = normalize(q_raw)
    y1 = across(p)
    z = in_chip(q)
    y2 = across(z)
    terms, weight = pair(p, q, jnp.eye(rows, dtype=jnp.float32))
    loss_p = jnp.sum(terms, axis=1)
    loss_q = jnp.sum(terms, axis=0)
    grad_p = dot(weight, q, 1, 0)
    grad_q = dot(weight, p, 0, 0)
    terms, weight = pair(z, q)
    loss_q = loss_q + jnp.sum(terms, axis=0)
    grad_q = grad_q + dot(weight, z, 0, 0)
    y1s = in_chip(y1)
    terms, weight = pair(y1s, y1)
    back = dot(weight, y1s, 0, 0)
    back_loss = jnp.pad(jnp.sum(terms, axis=0)[None, :], ((0, 7), (0, back.shape[1] - rows)))
    returned = across(jnp.concatenate([back, back_loss], axis=0))
    terms, weight = pair(p, y1)
    loss_p = loss_p + jnp.sum(terms, axis=1)
    grad_p = grad_p + dot(weight, y1, 1, 0)
    terms, weight = pair(y1s, q)
    loss_q = loss_q + jnp.sum(terms, axis=0)
    grad_q = grad_q + dot(weight, y1s, 0, 0)
    y2s = in_chip(y2)
    terms, weight = pair(p, y2)
    loss_p = loss_p + jnp.sum(terms, axis=1)
    grad_p = grad_p + dot(weight, y2, 1, 0)
    terms, weight = pair(y2s, q)
    loss_q = loss_q + jnp.sum(terms, axis=0)
    grad_q = grad_q + dot(weight, y2s, 0, 0)
    out_q = restore(q_raw, inv_q, grad_q)
    grad_p = grad_p + returned[:rows]
    loss_p = loss_p + returned[rows, :rows]
    out_p = restore(p_raw, inv_p, grad_p)
    loss_rows = jnp.where(even, loss_p, loss_q) / HOPS
    grad_image = jnp.where(even, out_p, out_q)
    text_gradient = jnp.where(even, out_q, out_p)
    return (loss_rows, grad_image, text_gradient)


def solution(mesh):
    placed = (P("blk", None), P("blk", None), P(), P())
    return jax.shard_map(
        body,
        mesh=mesh,
        in_specs=placed,
        out_specs=(P("blk"), P("blk", None), P("blk", None)),
        check_vma=False,
    )
```

```python
import jax
import jax.numpy as jnp
from jax import lax
from jax.sharding import PartitionSpec as P

HOPS = 4
EPS = 1e-06
HIGH = lax.Precision.HIGH


def across(value):
    count = lax.axis_size("blk")
    pairs = [(i, (i + 1 if i % 2 else i - 1) % count) for i in range(count)]
    return lax.ppermute(value, "blk", pairs)


def in_chip(value, even):
    count = lax.axis_size("blk")
    groups = [[i, i + 1] for i in range(0, count, 2)]
    both = lax.all_gather(value, "blk", axis_index_groups=groups)
    return jnp.where(even, both[1], both[0])


def normalize(raw):
    inverse_norm = lax.rsqrt(jnp.sum(raw * raw, axis=-1, keepdims=True) + EPS)
    return (raw * inverse_norm, inverse_norm)


def restore(raw, inverse_norm, grad):
    inner = jnp.sum(raw * grad, axis=-1, keepdims=True)
    return inverse_norm * grad - inverse_norm * inverse_norm * inverse_norm * inner * raw


def dot(a, b, ca, cb):
    return lax.dot_general(
        a, b, (((ca,), (cb,)), ((), ())), precision=HIGH, preferred_element_type=jnp.float32
    )


def body(picture_vectors, caption_vectors, sharpness_factor, additive_shift_term):
    rows = picture_vectors.shape[0]
    scale = sharpness_factor[0]
    shift = additive_shift_term[0]
    even = lax.axis_index("blk") % 2 == 0

    def pair(a, b, positive=None):
        shifted = scale * dot(a, b, 1, 1) + shift
        if positive is None:
            return jax.nn.softplus(shifted), scale * jax.nn.sigmoid(shifted)
        terms = jax.nn.softplus(shifted - 2.0 * positive * shifted)
        return terms, scale * (jax.nn.sigmoid(shifted) - positive)

    p_raw = jnp.where(even, picture_vectors, caption_vectors)
    q_raw = jnp.where(even, caption_vectors, picture_vectors)
    p, inv_p = normalize(p_raw)
    q, inv_q = normalize(q_raw)
    y1 = across(p)
    z = in_chip(q, even)
    y2 = across(z)
    y1s = in_chip(y1, even)
    terms, weight = pair(y1s, y1)
    back = dot(weight, y1s, 0, 0)
    back_loss = jnp.pad(jnp.sum(terms, axis=0)[None, :], ((0, 7), (0, back.shape[1] - rows)))
    sent = (jnp.concatenate([back, back_loss], axis=0))
    returned = across(sent)
    p, q, z, y1, y1s, sent = lax.optimization_barrier((p, q, z, y1, y1s, sent))
    terms, weight = pair(p, q, jnp.eye(rows, dtype=jnp.float32))
    loss_p = jnp.sum(terms, axis=1)
    loss_q = jnp.sum(terms, axis=0)
    grad_p = dot(weight, q, 1, 0)
    grad_q = dot(weight, p, 0, 0)
    terms, weight = pair(z, q)
    loss_q = loss_q + jnp.sum(terms, axis=0)
    grad_q = grad_q + dot(weight, z, 0, 0)
    terms, weight = pair(p, y1)
    loss_p = loss_p + jnp.sum(terms, axis=1)
    grad_p = grad_p + dot(weight, y1, 1, 0)
    terms, weight = pair(y1s, q)
    loss_q = loss_q + jnp.sum(terms, axis=0)
    grad_q = grad_q + dot(weight, y1s, 0, 0)
    y2s = in_chip(y2, even)
    terms, weight = pair(p, y2)
    loss_p = loss_p + jnp.sum(terms, axis=1)
    grad_p = grad_p + dot(weight, y2, 1, 0)
    terms, weight = pair(y2s, q)
    loss_q = loss_q + jnp.sum(terms, axis=0)
    grad_q = grad_q + dot(weight, y2s, 0, 0)
    out_q = restore(q_raw, inv_q, grad_q)
    grad_p = grad_p + returned[:rows]
    loss_p = loss_p + returned[rows, :rows]
    out_p = restore(p_raw, inv_p, grad_p)
    loss_rows = jnp.where(even, loss_p, loss_q) / HOPS
    grad_image = jnp.where(even, out_p, out_q)
    text_gradient = jnp.where(even, out_q, out_p)
    return (loss_rows, grad_image, text_gradient)


def solution(mesh):
    placed = (P("blk", None), P("blk", None), P(), P())
    return jax.shard_map(
        body,
        mesh=mesh,
        in_specs=placed,
        out_specs=(P("blk"), P("blk", None), P("blk", None)),
        check_vma=False,
    )
```

```python
import functools

import jax
import jax.numpy as jnp
from jax import lax
from jax.experimental import pallas as pl
from jax.experimental.pallas import tpu as pltpu
from jax.sharding import PartitionSpec as P

HOPS = 4
EPS = 1e-06
F32 = jnp.float32
BF16 = jnp.bfloat16
CHUNKS = 4
PAD = 8
VMEM_LIMIT = 24 * 1024 * 1024


def across(value):
    count = lax.axis_size("blk")
    pairs = [(i, (i + 1 if i % 2 else i - 1) % count) for i in range(count)]
    return lax.ppermute(value, "blk", pairs)


def in_chip(value):
    count = lax.axis_size("blk")
    return lax.ppermute(value, "blk", [(i, i ^ 1) for i in range(count)])


def split(value):
    high = value.astype(BF16)
    return high, (value - high.astype(F32)).astype(BF16)


def product(a, b, contract):
    def one(x, y):
        return lax.dot_general(x, y, (contract, ((), ())), preferred_element_type=F32)

    return one(a[0], b[0]) + (one(a[0], b[1]) + one(a[1], b[0]))


def logits(rows, others):
    return product(rows, others, ((1,), (1,)))


def pair_terms(logit, scale, shift, own=False):
    shifted = scale * logit + shift
    decay = jnp.exp(-jnp.abs(shifted))
    part = 1.0 / (1.0 + decay)
    sigmoid = jnp.where(shifted >= 0.0, part, decay * part)
    signed = shifted
    if own:
        shape = shifted.shape
        positive = lax.broadcasted_iota(jnp.int32, shape, 0) == lax.broadcasted_iota(jnp.int32, shape, 1)
        signed = jnp.where(positive, -shifted, shifted)
        sigmoid = sigmoid - jnp.where(positive, 1.0, 0.0)
    return jnp.maximum(signed, 0.0) + jnp.log1p(decay), scale * sigmoid


def spread(weight, others):
    return product(split(weight), others, ((1,), (0,)))


def step(number):
    return pl.when(lax.axis_index("blk") < (1 << 20) + number)


def row_sums(terms):
    sums = jnp.sum(terms, axis=1, keepdims=True)
    return jnp.transpose(jnp.broadcast_to(sums, (terms.shape[0], 128)))[:8]


def pick_kernel(odd_takes, image, text, unit, inverse, raw, sem):
    rows = raw.shape[0] // CHUNKS
    takes_image = lax.rem(lax.axis_index("blk"), 2) != odd_takes

    def copy(source, c):
        part = pl.ds(c * rows, rows)
        return pltpu.make_async_copy(source.at[part], raw.at[part], sem.at[c])

    @pl.when(takes_image)
    def _():
        for c in range(CHUNKS):
            copy(image, c).start()

    @pl.when(jnp.logical_not(takes_image))
    def _():
        for c in range(CHUNKS):
            copy(text, c).start()

    extra = unit.shape[0] - raw.shape[0]
    if extra:
        unit[raw.shape[0] :] = jnp.zeros((extra, raw.shape[1]), F32)
    for c in range(CHUNKS):
        copy(image, c).wait()
        part = pl.ds(c * rows, rows)
        value = raw[part]
        inv = lax.rsqrt(jnp.sum(value * value, axis=1, keepdims=True) + EPS)
        unit[part] = value * inv
        inverse[part] = jnp.broadcast_to(inv, (rows, 128))


def middle_kernel(scale, shift, y1, y1s, sent, tile, hi, lo):
    rows, width = y1s.shape

    @step(0)
    def _():
        hi[...], lo[...] = split(y1s[...])
        tile[...] = logits(split(y1[:rows]), (hi[...], lo[...]))

    @step(1)
    def _():
        terms, weight = pair_terms(tile[...], scale[0], shift[0])
        sent[:rows] = spread(weight, (hi[...], lo[...]))
        sent[rows:, :rows] = row_sums(terms)
        sent[rows:, rows:] = jnp.zeros((8, width - rows), F32)


def local_kernel(
    scale, shift, p_ref, q, z, y1, y1s, after, grad_p, grad_q, loss_p, loss_q, ph, plo, qh, qlo,
    zh, zl, yh, yl, sh, sl, tile_own, tile_z, tile_y, tile_s
):
    rows = q.shape[0]

    @step(0)
    def _():
        ph[...], plo[...] = split(p_ref[:rows])
        qh[...], qlo[...] = split(q[...])
        tile_own[...] = logits((ph[...], plo[...]), (qh[...], qlo[...]))
        zh[...], zl[...] = split(z[...])
        tile_z[...] = logits((qh[...], qlo[...]), (zh[...], zl[...]))
        yh[...], yl[...] = split(y1[:rows])
        tile_y[...] = logits((ph[...], plo[...]), (yh[...], yl[...]))
        sh[...], sl[...] = split(y1s[...])
        tile_s[...] = logits((qh[...], qlo[...]), (sh[...], sl[...]))

    @step(1)
    def _():
        terms_own, weight_own = pair_terms(tile_own[...], scale[0], shift[0], own=True)
        terms_y, weight_y = pair_terms(tile_y[...], scale[0], shift[0])
        loss_p[...] = terms_own + terms_y
        tile_own[...] = jnp.transpose(weight_own)
        grad_p[...] = spread(weight_own, (qh[...], qlo[...])) + spread(weight_y, (yh[...], yl[...]))
        loss_q[...] = jnp.transpose(terms_own)

    @step(2)
    def _():
        terms_z, weight_z = pair_terms(tile_z[...], scale[0], shift[0])
        terms_s, weight_s = pair_terms(tile_s[...], scale[0], shift[0])
        loss_q[...] += terms_z + terms_s
        grad_q[...] = (
            spread(tile_own[...], (ph[...], plo[...]))
            + spread(weight_z, (zh[...], zl[...]))
            + spread(weight_s, (sh[...], sl[...]))
        )


def restored(unit, inverse, grad):
    inner = jnp.sum(unit * grad, axis=1, keepdims=True)
    return inverse * (grad - inner * unit)


def put(value_ref, image_out, text_out, to_image, sem, c, rows):
    part = pl.ds(c * rows, rows)

    @pl.when(to_image)
    def _():
        pltpu.make_async_copy(value_ref.at[part], image_out.at[part], sem.at[c]).start()

    @pl.when(jnp.logical_not(to_image))
    def _():
        pltpu.make_async_copy(value_ref.at[part], text_out.at[part], sem.at[c]).start()


def finish(unit, inverse, grad, image_out, text_out, result, sem, to_image):
    rows = result.shape[0] // CHUNKS
    for c in range(CHUNKS):
        part = pl.ds(c * rows, rows)
        result[part] = restored(unit[part], inverse[part][:, :1], grad(part))
        put(result, image_out, text_out, to_image, sem, c, rows)
    for c in range(CHUNKS):
        part = pl.ds(c * rows, rows)
        pltpu.make_async_copy(result.at[part], image_out.at[part], sem.at[c]).wait()


def second_kernel(
    scale, shift, ph, plo, qh, qlo, y2, y2s, gp_in, gq_in, lp_in, lq_in, q, inv_q,
    image_out, text_out, grad_p, loss_p, loss_q, grad_q, yh, yl, sh, sl, tile_y, tile_s, result, sem
):
    rows = q.shape[0]

    @step(0)
    def _():
        yh[...], yl[...] = split(y2[:rows])
        tile_y[...] = logits((ph[...], plo[...]), (yh[...], yl[...]))
        sh[...], sl[...] = split(y2s[...])
        tile_s[...] = logits((qh[...], qlo[...]), (sh[...], sl[...]))

    @step(1)
    def _():
        terms_s, weight_s = pair_terms(tile_s[...], scale[0], shift[0])
        grad_q[...] = gq_in[...] + spread(weight_s, (sh[...], sl[...]))
        terms_y, weight_y = pair_terms(tile_y[...], scale[0], shift[0])
        grad_p[...] = gp_in[...] + spread(weight_y, (yh[...], yl[...]))
        loss_p[...] = row_sums(lp_in[...] + terms_y)
        loss_q[...] = row_sums(lq_in[...] + terms_s)

    odd = lax.rem(lax.axis_index("blk"), 2) == 1
    finish(q, inv_q, lambda part: grad_q[part], image_out, text_out, result, sem, odd)


def last_kernel(
    gp_in, returned, p, inv_p, loss_p, loss_q, image_in, text_in, loss, image_out, text_out, result, sem
):
    rows = result.shape[0]
    even = lax.rem(lax.axis_index("blk"), 2) == 0
    total = jnp.where(even, loss_p[:1] + returned[rows : rows + 1, :rows], loss_q[:1])
    loss[...] = total * (1.0 / HOPS)
    finish(
        p, inv_p, lambda part: gp_in[part] + returned[part], image_out, text_out, result, sem, even
    )


def call(kernel, ins, outs, scratch=(), aliases=None):
    arrays, specs = [], []
    for array, place in ins:
        specs.append(pl.BlockSpec(memory_space=place))
        arrays.append(pltpu.with_memory_space_constraint(array, place) if place in (pltpu.VMEM, pltpu.HBM) else array)
    return pl.pallas_call(
        kernel,
        out_shape=[o for o, _ in outs],
        in_specs=specs,
        out_specs=[pl.BlockSpec(memory_space=place) for _, place in outs],
        scratch_shapes=list(scratch),
        input_output_aliases=aliases or {},
        compiler_params=pltpu.CompilerParams(vmem_limit_bytes=VMEM_LIMIT),
        cost_estimate=pl.CostEstimate(flops=0, transcendentals=0, bytes_accessed=0),
    )(*arrays)


def body(picture_vectors, caption_vectors, sharpness_factor, additive_shift_term):
    rows, width = picture_vectors.shape
    block = (rows, width)
    vm, hbm, sm, anywhere = pltpu.VMEM, pltpu.HBM, pltpu.SMEM, pl.ANY

    def fast(shape=block, dtype=F32):
        return (pltpu.VMEM(shape, dtype), vm)

    scalars = [(sharpness_factor, sm), (additive_shift_term, sm)]

    def v(*arrays):
        return [(a, vm) for a in arrays]

    def pick(odd_takes, taken):
        return call(
            functools.partial(pick_kernel, odd_takes),
            [(picture_vectors, hbm), (caption_vectors, hbm)],
            [fast((taken, width)), fast((rows, 128))],
            [pltpu.VMEM(block, F32), pltpu.SemaphoreType.DMA((CHUNKS,))],
        )

    line, square, half = (8, rows), (rows, rows), pltpu.VMEM(block, BF16)
    p, inv_p = pick(1, rows + PAD)
    y1 = across(p)
    q, inv_q = pick(0, rows)
    z = in_chip(q)
    y2 = across(jnp.pad(z, ((0, PAD), (0, 0))))
    y1s = in_chip(y1[:rows])
    (sent,) = call(
        middle_kernel,
        scalars + v(y1, y1s),
        [fast((rows + 8, width))],
        [pltpu.VMEM(square, F32), half, half],
    )
    returned = across(sent)
    halves = [fast(block, BF16)] * 4
    grad_p, grad_q, loss_p, loss_q, ph, plo, qh, qlo = call(
        local_kernel,
        scalars + v(p, q, z, y1, y1s) + [(sent, anywhere)],
        [fast(), fast(), fast(square), fast(square)] + halves,
        [half] * 6 + [pltpu.VMEM(square, F32)] * 4,
    )
    y2s = in_chip(y2[:rows])
    whole = (jax.ShapeDtypeStruct(block, F32), hbm)
    out_scratch = [pltpu.VMEM(block, F32), pltpu.SemaphoreType.DMA((CHUNKS,))]
    image_out, text_out, grad_p, loss_p, loss_q = call(
        second_kernel,
        scalars + v(ph, plo, qh, qlo, y2, y2s, grad_p, grad_q, loss_p, loss_q, q, inv_q),
        [whole, whole, fast(), fast(line), fast(line)],
        [pltpu.VMEM(block, F32)] + [half] * 4 + [pltpu.VMEM(square, F32)] * 2 + out_scratch,
    )
    loss, grad_image, text_gradient = call(
        last_kernel,
        v(grad_p, returned, p, inv_p, loss_p, loss_q) + [(image_out, hbm), (text_out, hbm)],
        [(jax.ShapeDtypeStruct((1, rows), F32), vm), whole, whole],
        out_scratch,
        {6: 1, 7: 2},
    )
    return (loss.reshape(rows), grad_image, text_gradient)


def solution(mesh):
    placed = (P("blk", None), P("blk", None), P(), P())
    return jax.shard_map(
        body,
        mesh=mesh,
        in_specs=placed,
        out_specs=(P("blk"), P("blk", None), P("blk", None)),
        check_vma=False,
    )
```

```python
import functools

import jax
import jax.numpy as jnp
from jax import lax
from jax.experimental import pallas as pl
from jax.experimental.pallas import tpu as pltpu
from jax.sharding import PartitionSpec as P

HOPS = 4
EPS = 1e-06
F32 = jnp.float32
BF16 = jnp.bfloat16
CHUNKS = 4
PAD = 8
COST_Q = 8000000
COST_OWN = 8000000
VMEM_LIMIT = 24 * 1024 * 1024


def across(value):
    count = lax.axis_size("blk")
    pairs = [(i, (i + 1 if i % 2 else i - 1) % count) for i in range(count)]
    return lax.ppermute(value, "blk", pairs)


def in_chip(value):
    count = lax.axis_size("blk")
    return lax.ppermute(value, "blk", [(i, i ^ 1) for i in range(count)])


def split(value):
    high = value.astype(BF16)
    return high, (value - high.astype(F32)).astype(BF16)


def product(a, b, contract):
    def one(x, y):
        return lax.dot_general(x, y, (contract, ((), ())), preferred_element_type=F32)

    return one(a[0], b[0]) + (one(a[0], b[1]) + one(a[1], b[0]))


def logits(rows, others):
    return product(rows, others, ((1,), (1,)))


def pair_terms(logit, scale, shift, own=False):
    shifted = scale * logit + shift
    decay = jnp.exp(-jnp.abs(shifted))
    part = 1.0 / (1.0 + decay)
    sigmoid = jnp.where(shifted >= 0.0, part, decay * part)
    signed = shifted
    if own:
        shape = shifted.shape
        positive = lax.broadcasted_iota(jnp.int32, shape, 0) == lax.broadcasted_iota(jnp.int32, shape, 1)
        signed = jnp.where(positive, -shifted, shifted)
        sigmoid = sigmoid - jnp.where(positive, 1.0, 0.0)
    return jnp.maximum(signed, 0.0) + jnp.log1p(decay), scale * sigmoid


def spread(weight, others):
    return product(split(weight), others, ((1,), (0,)))


def step(number):
    return pl.when(lax.axis_index("blk") < (1 << 20) + number)


def row_sums(terms):
    sums = jnp.sum(terms, axis=1, keepdims=True)
    return jnp.transpose(jnp.broadcast_to(sums, (terms.shape[0], 128)))[:8]


def pick_kernel(odd_takes, image, text, unit, inverse, raw, sem):
    rows = raw.shape[0] // CHUNKS
    takes_image = lax.rem(lax.axis_index("blk"), 2) != odd_takes

    def copy(source, c):
        part = pl.ds(c * rows, rows)
        return pltpu.make_async_copy(source.at[part], raw.at[part], sem.at[c])

    @pl.when(takes_image)
    def _():
        for c in range(CHUNKS):
            copy(image, c).start()

    @pl.when(jnp.logical_not(takes_image))
    def _():
        for c in range(CHUNKS):
            copy(text, c).start()

    extra = unit.shape[0] - raw.shape[0]
    if extra:
        unit[raw.shape[0] :] = jnp.zeros((extra, raw.shape[1]), F32)
    for c in range(CHUNKS):
        copy(image, c).wait()
        part = pl.ds(c * rows, rows)
        value = raw[part]
        inv = lax.rsqrt(jnp.sum(value * value, axis=1, keepdims=True) + EPS)
        unit[part] = value * inv
        inverse[part] = jnp.broadcast_to(inv, (rows, 128))


def middle_kernel(scale, shift, y1, y1s, sent, tile, yh, yl, sh, sl):
    rows, width = yh.shape

    @step(0)
    def _():
        sh[...], sl[...] = split(y1s[...])
        yh[...], yl[...] = split(y1[: yh.shape[0]])
        tile[...] = logits((yh[...], yl[...]), (sh[...], sl[...]))

    @step(1)
    def _():
        terms, weight = pair_terms(tile[...], scale[0], shift[0])
        sent[:rows] = spread(weight, (sh[...], sl[...]))
        sent[rows:, :rows] = row_sums(terms)
        sent[rows:, rows:] = jnp.zeros((8, width - rows), F32)


def own_kernel(
    scale, shift, p, q, z, grad_p, grad_q, loss_p, loss_q, ph, plo, qh, qlo, zh, zl, tile_own, tile_z
):
    @step(0)
    def _():
        ph[...], plo[...] = split(p[: ph.shape[0]])
        qh[...], qlo[...] = split(q[...])
        tile_own[...] = logits((ph[...], plo[...]), (qh[...], qlo[...]))
        zh[...], zl[...] = split(z[...])
        tile_z[...] = logits((qh[...], qlo[...]), (zh[...], zl[...]))

    @step(1)
    def _():
        terms, weight = pair_terms(tile_own[...], scale[0], shift[0], own=True)
        terms_z, weight_z = pair_terms(tile_z[...], scale[0], shift[0])
        loss_p[...] = terms
        loss_q[...] = jnp.transpose(terms) + terms_z
        grad_p[...] = spread(weight, (qh[...], qlo[...]))
        grad_q[...] = spread(jnp.transpose(weight), (ph[...], plo[...])) + spread(weight_z, (zh[...], zl[...]))


def first_kernel(
    scale, shift, ph, plo, qh, qlo, y1, y1s, y2, gp_in, gq_in, lp_in, lq_in, after,
    grad_p, grad_q, loss_p, loss_q, yh, yl, sh, sl, wh, wl, tile_y, tile_s, tile_w
):
    rows = yh.shape[0]

    @step(0)
    def _():
        yh[...], yl[...] = split(y1[: yh.shape[0]])
        tile_y[...] = logits((ph[...], plo[...]), (yh[...], yl[...]))
        sh[...], sl[...] = split(y1s[...])
        tile_s[...] = logits((qh[...], qlo[...]), (sh[...], sl[...]))
        wh[...], wl[...] = split(y2[:rows])
        tile_w[...] = logits((ph[...], plo[...]), (wh[...], wl[...]))

    @step(1)
    def _():
        terms_y, weight_y = pair_terms(tile_y[...], scale[0], shift[0])
        terms_s, weight_s = pair_terms(tile_s[...], scale[0], shift[0])
        terms_w, weight_w = pair_terms(tile_w[...], scale[0], shift[0])
        loss_p[...] = row_sums(lp_in[...] + terms_y + terms_w)
        loss_q[...] = lq_in[...] + terms_s
        grad_p[...] = gp_in[...] + spread(weight_y, (yh[...], yl[...])) + spread(weight_w, (wh[...], wl[...]))
        grad_q[...] = gq_in[...] + spread(weight_s, (sh[...], sl[...]))


def restored(unit, inverse, grad):
    inner = jnp.sum(unit * grad, axis=1, keepdims=True)
    return inverse * (grad - inner * unit)


def put(value_ref, image_out, text_out, to_image, sem, c, rows):
    part = pl.ds(c * rows, rows)

    @pl.when(to_image)
    def _():
        pltpu.make_async_copy(value_ref.at[part], image_out.at[part], sem.at[c]).start()

    @pl.when(jnp.logical_not(to_image))
    def _():
        pltpu.make_async_copy(value_ref.at[part], text_out.at[part], sem.at[c]).start()


def finish(unit, inverse, grad, image_out, text_out, result, sem, to_image):
    rows = result.shape[0] // CHUNKS
    for c in range(CHUNKS):
        part = pl.ds(c * rows, rows)
        result[part] = restored(unit[part], inverse[part][:, :1], grad(part))
        put(result, image_out, text_out, to_image, sem, c, rows)
    for c in range(CHUNKS):
        part = pl.ds(c * rows, rows)
        pltpu.make_async_copy(result.at[part], image_out.at[part], sem.at[c]).wait()


def second_kernel(
    scale, shift, qh, qlo, y2s, gq_in, lq_in, q, inv_q,
    image_out, text_out, loss_q, grad_q, sh, sl, tile_s, result, sem
):
    @step(0)
    def _():
        sh[...], sl[...] = split(y2s[...])
        tile_s[...] = logits((qh[...], qlo[...]), (sh[...], sl[...]))

    @step(1)
    def _():
        terms, weight = pair_terms(tile_s[...], scale[0], shift[0])
        grad_q[...] = gq_in[...] + spread(weight, (sh[...], sl[...]))
        loss_q[...] = row_sums(lq_in[...] + terms)

    odd = lax.rem(lax.axis_index("blk"), 2) == 1
    finish(q, inv_q, lambda part: grad_q[part], image_out, text_out, result, sem, odd)


def last_kernel(
    gp_in, returned, p, inv_p, loss_p, loss_q, image_in, text_in, loss, image_out, text_out, result, sem
):
    rows = result.shape[0]
    even = lax.rem(lax.axis_index("blk"), 2) == 0
    total = jnp.where(even, loss_p[:1] + returned[rows : rows + 1, :rows], loss_q[:1])
    loss[...] = total * (1.0 / HOPS)
    finish(
        p, inv_p, lambda part: gp_in[part] + returned[part], image_out, text_out, result, sem, even
    )


def call(kernel, ins, outs, scratch=(), aliases=None, cost=0):
    arrays, specs = [], []
    for array, place in ins:
        specs.append(pl.BlockSpec(memory_space=place))
        arrays.append(pltpu.with_memory_space_constraint(array, place) if place in (pltpu.VMEM, pltpu.HBM) else array)
    return pl.pallas_call(
        kernel,
        out_shape=[o for o, _ in outs],
        in_specs=specs,
        out_specs=[pl.BlockSpec(memory_space=place) for _, place in outs],
        scratch_shapes=list(scratch),
        input_output_aliases=aliases or {},
        compiler_params=pltpu.CompilerParams(vmem_limit_bytes=VMEM_LIMIT),
        cost_estimate=pl.CostEstimate(flops=0, transcendentals=0, bytes_accessed=cost),
    )(*arrays)


def body(picture_vectors, caption_vectors, sharpness_factor, additive_shift_term):
    rows, width = picture_vectors.shape
    block = (rows, width)
    vm, hbm, sm, anywhere = pltpu.VMEM, pltpu.HBM, pltpu.SMEM, pl.ANY

    def fast(shape=block, dtype=F32):
        return (pltpu.VMEM(shape, dtype), vm)

    scalars = [(sharpness_factor, sm), (additive_shift_term, sm)]

    def v(*arrays):
        return [(a, vm) for a in arrays]

    def pick(odd_takes, taken, cost):
        return call(
            functools.partial(pick_kernel, odd_takes),
            [(picture_vectors, hbm), (caption_vectors, hbm)],
            [fast((taken, width)), fast((rows, 128))],
            [pltpu.VMEM(block, F32), pltpu.SemaphoreType.DMA((CHUNKS,))],
            cost=cost,
        )

    line, square, half = (8, rows), (rows, rows), pltpu.VMEM(block, BF16)
    tile = pltpu.VMEM(square, F32)
    p, inv_p = pick(1, rows + PAD, 0)
    y1 = across(p)
    q, inv_q = pick(0, rows, COST_Q)
    z = in_chip(q)
    y2 = across(jnp.pad(z, ((0, PAD), (0, 0))))
    grad_p, grad_q, loss_p, loss_q, ph, plo, qh, qlo = call(
        own_kernel,
        scalars + v(p, q, z),
        [fast(), fast(), fast(square), fast(square)] + [fast(block, BF16)] * 4,
        [half] * 2 + [tile] * 2,
        cost=COST_OWN,
    )
    y1, grad_p = lax.optimization_barrier((y1, grad_p))
    y1s = in_chip(y1[:rows])
    (sent,) = call(
        middle_kernel,
        scalars + v(y1, y1s),
        [fast((rows + 8, width))],
        [tile] + [half] * 4,
    )
    returned = across(sent)
    y2s = in_chip(y2[:rows])
    grad_p, grad_q, loss_p, loss_q = call(
        first_kernel,
        scalars
        + v(ph, plo, qh, qlo, y1, y1s, y2, grad_p, grad_q, loss_p, loss_q)
        + [(sent, anywhere)],
        [fast(), fast(), fast(line), fast(square)],
        [half] * 6 + [tile] * 3,
    )
    whole = (jax.ShapeDtypeStruct(block, F32), hbm)
    out_scratch = [pltpu.VMEM(block, F32), pltpu.SemaphoreType.DMA((CHUNKS,))]
    image_out, text_out, loss_q = call(
        second_kernel,
        scalars + v(qh, qlo, y2s, grad_q, loss_q, q, inv_q),
        [whole, whole, fast(line)],
        [pltpu.VMEM(block, F32)] + [half] * 2 + [tile] + out_scratch,
    )
    loss, grad_image, text_gradient = call(
        last_kernel,
        v(grad_p, returned, p, inv_p, loss_p, loss_q) + [(image_out, hbm), (text_out, hbm)],
        [(jax.ShapeDtypeStruct((1, rows), F32), vm), whole, whole],
        out_scratch,
        {6: 1, 7: 2},
    )
    return (loss.reshape(rows), grad_image, text_gradient)


def solution(mesh):
    placed = (P("blk", None), P("blk", None), P(), P())
    return jax.shard_map(
        body,
        mesh=mesh,
        in_specs=placed,
        out_specs=(P("blk"), P("blk", None), P("blk", None)),
        check_vma=False,
    )
```

```python
import functools

import jax
import jax.numpy as jnp
from jax import lax
from jax.experimental import pallas as pl
from jax.experimental.pallas import tpu as pltpu
from jax.sharding import PartitionSpec as P

HOPS = 4
EPS = 1e-06
F32 = jnp.float32
BF16 = jnp.bfloat16
CHUNKS = 4
PAD = 8
COST_Q = 8000000
COST_OWN = 8000000
VMEM_LIMIT = 24 * 1024 * 1024


def across(value):
    count = lax.axis_size("blk")
    pairs = [(i, (i + 1 if i % 2 else i - 1) % count) for i in range(count)]
    return lax.ppermute(value, "blk", pairs)


def in_chip(value):
    count = lax.axis_size("blk")
    return lax.ppermute(value, "blk", [(i, i ^ 1) for i in range(count)])


def split(value):
    high = value.astype(BF16)
    return high, (value - high.astype(F32)).astype(BF16)


def product(a, b, contract):
    def one(x, y):
        return lax.dot_general(x, y, (contract, ((), ())), preferred_element_type=F32)

    return one(a[0], b[0]) + (one(a[0], b[1]) + one(a[1], b[0]))


def logits(rows, others):
    return product(rows, others, ((1,), (1,)))


def pair_terms(logit, scale, shift, own=False):
    shifted = scale * logit + shift
    decay = jnp.exp(-jnp.abs(shifted))
    part = 1.0 / (1.0 + decay)
    sigmoid = jnp.where(shifted >= 0.0, part, decay * part)
    signed = shifted
    if own:
        shape = shifted.shape
        positive = lax.broadcasted_iota(jnp.int32, shape, 0) == lax.broadcasted_iota(jnp.int32, shape, 1)
        signed = jnp.where(positive, -shifted, shifted)
        sigmoid = sigmoid - jnp.where(positive, 1.0, 0.0)
    return jnp.maximum(signed, 0.0) + jnp.log1p(decay), scale * sigmoid


def spread(weight, others):
    return product(split(weight), others, ((1,), (0,)))


def step(number):
    return pl.when(lax.axis_index("blk") < (1 << 20) + number)


def row_sums(terms):
    sums = jnp.sum(terms, axis=1, keepdims=True)
    return jnp.transpose(jnp.broadcast_to(sums, (terms.shape[0], 128)))[:8]


def pick_kernel(odd_takes, image, text, unit, inverse, raw, sem):
    rows = raw.shape[0] // CHUNKS
    takes_image = lax.rem(lax.axis_index("blk"), 2) != odd_takes

    def copy(source, c):
        part = pl.ds(c * rows, rows)
        return pltpu.make_async_copy(source.at[part], raw.at[part], sem.at[c])

    @pl.when(takes_image)
    def _():
        for c in range(CHUNKS):
            copy(image, c).start()

    @pl.when(jnp.logical_not(takes_image))
    def _():
        for c in range(CHUNKS):
            copy(text, c).start()

    extra = unit.shape[0] - raw.shape[0]
    if extra:
        unit[raw.shape[0] :] = jnp.zeros((extra, raw.shape[1]), F32)
    for c in range(CHUNKS):
        copy(image, c).wait()
        part = pl.ds(c * rows, rows)
        value = raw[part]
        inv = lax.rsqrt(jnp.sum(value * value, axis=1, keepdims=True) + EPS)
        unit[part] = value * inv
        inverse[part] = jnp.broadcast_to(inv, (rows, 128))


def middle_kernel(scale, shift, y1, y1s, sent, tile, yh, yl, sh, sl):
    rows, width = yh.shape

    @step(0)
    def _():
        sh[...], sl[...] = split(y1s[...])
        yh[...], yl[...] = split(y1[: yh.shape[0]])
        tile[...] = logits((yh[...], yl[...]), (sh[...], sl[...]))

    @step(1)
    def _():
        terms, weight = pair_terms(tile[...], scale[0], shift[0])
        sent[:rows] = spread(weight, (sh[...], sl[...]))
        sent[rows:, :rows] = row_sums(terms)
        sent[rows:, rows:] = jnp.zeros((8, width - rows), F32)


def own_kernel(
    scale, shift, p, q, z, grad_p, grad_q, loss_p, loss_q, ph, plo, qh, qlo, zh, zl, tile_own, tile_z
):
    @step(0)
    def _():
        ph[...], plo[...] = split(p[: ph.shape[0]])
        qh[...], qlo[...] = split(q[...])
        tile_own[...] = logits((ph[...], plo[...]), (qh[...], qlo[...]))
        zh[...], zl[...] = split(z[...])
        tile_z[...] = logits((qh[...], qlo[...]), (zh[...], zl[...]))

    @step(1)
    def _():
        terms, weight = pair_terms(tile_own[...], scale[0], shift[0], own=True)
        terms_z, weight_z = pair_terms(tile_z[...], scale[0], shift[0])
        loss_p[...] = terms
        loss_q[...] = jnp.transpose(terms) + terms_z
        grad_p[...] = spread(weight, (qh[...], qlo[...]))
        grad_q[...] = spread(jnp.transpose(weight), (ph[...], plo[...])) + spread(weight_z, (zh[...], zl[...]))


def add_first(scale, shift, ph, plo, qh, qlo, y1, y1s, gp_in, gq_in, lp_in, lq_in, grad_p, grad_q, loss_p, loss_q, scratch):
    yh, yl, sh, sl, tile_y, tile_s = scratch

    def logit_part():
        yh[...], yl[...] = split(y1[: yh.shape[0]])
        tile_y[...] = logits((ph[...], plo[...]), (yh[...], yl[...]))
        sh[...], sl[...] = split(y1s[...])
        tile_s[...] = logits((qh[...], qlo[...]), (sh[...], sl[...]))

    def gradient_part():
        terms_y, weight_y = pair_terms(tile_y[...], scale[0], shift[0])
        terms_s, weight_s = pair_terms(tile_s[...], scale[0], shift[0])
        loss_p[...] = lp_in[...] + terms_y
        loss_q[...] = lq_in[...] + terms_s
        grad_p[...] = gp_in[...] + spread(weight_y, (yh[...], yl[...]))
        grad_q[...] = gq_in[...] + spread(weight_s, (sh[...], sl[...]))

    return logit_part, gradient_part


def odd_first_kernel(
    scale, shift, ph, plo, qh, qlo, y1, y1s, gp_in, gq_in, lp_in, lq_in, after, grad_p, grad_q, loss_p, loss_q, *scratch
):
    parts = add_first(
        scale, shift, ph, plo, qh, qlo, y1, y1s, gp_in, gq_in, lp_in, lq_in, grad_p, grad_q, loss_p, loss_q, scratch
    )
    for part in parts:
        pl.when(lax.rem(lax.axis_index("blk"), 2) == 1)(part)


def even_first_kernel(
    scale, shift, ph, plo, qh, qlo, y1, y1s, y2, gp_in, gq_in, lp_in, lq_in, grad_p, grad_q, loss_p, loss_q,
    wh, wl, tile_w, *scratch
):
    parts = add_first(
        scale, shift, ph, plo, qh, qlo, y1, y1s, gp_in, gq_in, lp_in, lq_in, grad_p, grad_q, loss_p, loss_q, scratch
    )
    for part in parts:
        pl.when(lax.rem(lax.axis_index("blk"), 2) == 0)(part)

    @step(0)
    def _():
        wh[...], wl[...] = split(y2[: wh.shape[0]])
        tile_w[...] = logits((ph[...], plo[...]), (wh[...], wl[...]))

    @step(1)
    def _():
        terms, weight = pair_terms(tile_w[...], scale[0], shift[0])
        loss_p[...] = lp_in[...] + terms
        grad_p[...] = gp_in[...] + spread(weight, (wh[...], wl[...]))


def restored(unit, inverse, grad):
    inner = jnp.sum(unit * grad, axis=1, keepdims=True)
    return inverse * (grad - inner * unit)


def put(value_ref, image_out, text_out, to_image, sem, c, rows):
    part = pl.ds(c * rows, rows)

    @pl.when(to_image)
    def _():
        pltpu.make_async_copy(value_ref.at[part], image_out.at[part], sem.at[c]).start()

    @pl.when(jnp.logical_not(to_image))
    def _():
        pltpu.make_async_copy(value_ref.at[part], text_out.at[part], sem.at[c]).start()


def finish(unit, inverse, grad, image_out, text_out, result, sem, to_image):
    rows = result.shape[0] // CHUNKS
    for c in range(CHUNKS):
        part = pl.ds(c * rows, rows)
        result[part] = restored(unit[part], inverse[part][:, :1], grad(part))
        put(result, image_out, text_out, to_image, sem, c, rows)
    for c in range(CHUNKS):
        part = pl.ds(c * rows, rows)
        pltpu.make_async_copy(result.at[part], image_out.at[part], sem.at[c]).wait()


def second_kernel(
    scale, shift, qh, qlo, y2s, gq_in, lq_in, lp_in, q, inv_q,
    image_out, text_out, loss_q, loss_p, sh, sl, tile_s, result, sem
):
    @step(0)
    def _():
        sh[...], sl[...] = split(y2s[...])
        tile_s[...] = logits((qh[...], qlo[...]), (sh[...], sl[...]))

    odd = lax.rem(lax.axis_index("blk"), 2) == 1
    rows = result.shape[0] // 2
    for h in range(2):
        part = pl.ds(h * rows, rows)

        @step(1 + h)
        def _():
            terms, weight = pair_terms(tile_s[part], scale[0], shift[0])
            grad = gq_in[part] + spread(weight, (sh[...], sl[...]))
            result[part] = restored(q[part], inv_q[part][:, :1], grad)
            tile_s[part] = lq_in[part] + terms
            put(result, image_out, text_out, odd, sem, h, rows)

    loss_q[...] = row_sums(tile_s[...])
    loss_p[...] = row_sums(lp_in[...])
    for h in range(2):
        part = pl.ds(h * rows, rows)
        pltpu.make_async_copy(result.at[part], image_out.at[part], sem.at[h]).wait()


def last_kernel(
    gp_in, returned, p, inv_p, loss_p, loss_q, image_in, text_in, loss, image_out, text_out, result, sem, line, line_sem
):
    rows = result.shape[0]
    even = lax.rem(lax.axis_index("blk"), 2) == 0
    total = jnp.where(even, loss_p[:1] + returned[rows : rows + 1, :rows], loss_q[:1])
    line[...] = total * (1.0 / HOPS)
    copy = pltpu.make_async_copy(line, loss, line_sem)
    copy.start()
    finish(
        p, inv_p, lambda part: gp_in[part] + returned[part], image_out, text_out, result, sem, even
    )
    copy.wait()


def call(kernel, ins, outs, scratch=(), aliases=None, cost=0):
    arrays, specs = [], []
    for array, place in ins:
        specs.append(pl.BlockSpec(memory_space=place))
        arrays.append(pltpu.with_memory_space_constraint(array, place) if place in (pltpu.VMEM, pltpu.HBM) else array)
    return pl.pallas_call(
        kernel,
        out_shape=[o for o, _ in outs],
        in_specs=specs,
        out_specs=[pl.BlockSpec(memory_space=place) for _, place in outs],
        scratch_shapes=list(scratch),
        input_output_aliases=aliases or {},
        compiler_params=pltpu.CompilerParams(vmem_limit_bytes=VMEM_LIMIT),
        cost_estimate=pl.CostEstimate(flops=0, transcendentals=0, bytes_accessed=cost),
    )(*arrays)


def body(picture_vectors, caption_vectors, sharpness_factor, additive_shift_term):
    rows, width = picture_vectors.shape
    block = (rows, width)
    vm, hbm, sm, anywhere = pltpu.VMEM, pltpu.HBM, pltpu.SMEM, pl.ANY

    def fast(shape=block, dtype=F32):
        return (pltpu.VMEM(shape, dtype), vm)

    scalars = [(sharpness_factor, sm), (additive_shift_term, sm)]

    def v(*arrays):
        return [(a, vm) for a in arrays]

    def pick(odd_takes, taken, cost):
        return call(
            functools.partial(pick_kernel, odd_takes),
            [(picture_vectors, hbm), (caption_vectors, hbm)],
            [fast((taken, width)), fast((rows, 128))],
            [pltpu.VMEM(block, F32), pltpu.SemaphoreType.DMA((CHUNKS,))],
            cost=cost,
        )

    line, square, half = (8, rows), (rows, rows), pltpu.VMEM(block, BF16)
    tile = pltpu.VMEM(square, F32)
    p, inv_p = pick(1, rows + PAD, 0)
    y1 = across(p)
    q, inv_q = pick(0, rows, COST_Q)
    z = in_chip(q)
    y2 = across(jnp.pad(z, ((0, PAD), (0, 0))))
    grad_p, grad_q, loss_p, loss_q, ph, plo, qh, qlo = call(
        own_kernel,
        scalars + v(p, q, z),
        [fast(), fast(), fast(square), fast(square)] + [fast(block, BF16)] * 4,
        [half] * 2 + [tile] * 2,
        cost=COST_OWN,
    )
    y1, grad_p = lax.optimization_barrier((y1, grad_p))
    y1s = in_chip(y1[:rows])
    (sent,) = call(
        middle_kernel,
        scalars + v(y1, y1s),
        [fast((rows + 8, width))],
        [tile] + [half] * 4,
    )
    returned = across(sent)
    state = [grad_p, grad_q, loss_p, loss_q]
    outs = [fast(), fast(), fast(square), fast(square)]
    scratch = [half] * 4 + [tile] * 2
    state = call(
        odd_first_kernel,
        scalars + v(ph, plo, qh, qlo, y1, y1s, *state) + [(sent, anywhere)],
        outs,
        scratch,
        {8 + i: i for i in range(4)},
    )
    y2, state = lax.optimization_barrier((y2, state))
    y2s = in_chip(y2[:rows])
    grad_p, grad_q, loss_p, loss_q = call(
        even_first_kernel,
        scalars + v(ph, plo, qh, qlo, y1, y1s, y2, *state),
        outs,
        [half, half, tile] + scratch,
        {9 + i: i for i in range(4)},
    )
    whole = (jax.ShapeDtypeStruct(block, F32), hbm)
    out_scratch = [pltpu.VMEM(block, F32), pltpu.SemaphoreType.DMA((CHUNKS,))]
    image_out, text_out, loss_q, loss_p = call(
        second_kernel,
        scalars + v(qh, qlo, y2s, grad_q, loss_q, loss_p, q, inv_q),
        [whole, whole, fast(line), fast(line)],
        [half] * 2 + [tile] + out_scratch,
    )
    loss, grad_image, text_gradient = call(
        last_kernel,
        v(grad_p, returned, p, inv_p, loss_p, loss_q) + [(image_out, hbm), (text_out, hbm)],
        [(jax.ShapeDtypeStruct((1, rows), F32), hbm), whole, whole],
        out_scratch + [pltpu.VMEM((1, rows), F32), pltpu.SemaphoreType.DMA],
        {6: 1, 7: 2},
    )
    return (loss.reshape(rows), grad_image, text_gradient)


def solution(mesh):
    placed = (P("blk", None), P("blk", None), P(), P())
    return jax.shard_map(
        body,
        mesh=mesh,
        in_specs=placed,
        out_specs=(P("blk"), P("blk", None), P("blk", None)),
        check_vma=False,
    )
```

```python
import functools

import jax
import jax.numpy as jnp
from jax import lax
from jax.experimental import pallas as pl
from jax.experimental.pallas import tpu as pltpu
from jax.sharding import PartitionSpec as P

HOPS = 4
EPS = 1e-06
F32 = jnp.float32
BF16 = jnp.bfloat16
CHUNKS = 4
PAD = 8
COST_Q = 8000000
COST_OWN = 8000000
COST_SPLIT = 4000000
VMEM_LIMIT = 20 * 1024 * 1024


def across(value):
    count = lax.axis_size("blk")
    pairs = [(i, (i + 1 if i % 2 else i - 1) % count) for i in range(count)]
    return lax.ppermute(value, "blk", pairs)


def in_chip(value):
    count = lax.axis_size("blk")
    return lax.ppermute(value, "blk", [(i, i ^ 1) for i in range(count)])


def in_chip_in_halves(value):
    half = value.shape[0] // 2
    return jnp.concatenate([in_chip(value[:half]), in_chip(value[half:])], axis=0)


def split(value):
    high = value.astype(BF16)
    return high, (value - high.astype(F32)).astype(BF16)


def product(a, b, contract):
    def one(x, y):
        return lax.dot_general(x, y, (contract, ((), ())), preferred_element_type=F32)

    return one(a[0], b[0]) + (one(a[0], b[1]) + one(a[1], b[0]))


def logits(rows, others):
    return product(rows, others, ((1,), (1,)))


def pair_terms(logit, scale, shift, own=False):
    shifted = scale * logit + shift
    decay = jnp.exp(-jnp.abs(shifted))
    part = 1.0 / (1.0 + decay)
    sigmoid = jnp.where(shifted >= 0.0, part, decay * part)
    signed = shifted
    if own:
        shape = shifted.shape
        positive = lax.broadcasted_iota(jnp.int32, shape, 0) == lax.broadcasted_iota(jnp.int32, shape, 1)
        signed = jnp.where(positive, -shifted, shifted)
        sigmoid = sigmoid - jnp.where(positive, 1.0, 0.0)
    return jnp.maximum(signed, 0.0) + jnp.log1p(decay), scale * sigmoid


def spread(weight, others):
    return product(split(weight), others, ((1,), (0,)))


def step(number):
    return pl.when(lax.axis_index("blk") < (1 << 20) + number)


def row_sums(terms):
    sums = jnp.sum(terms, axis=1, keepdims=True)
    return jnp.transpose(jnp.broadcast_to(sums, (terms.shape[0], 128)))[:8]


def inverse_norm(value):
    return lax.rsqrt(jnp.sum(value * value, axis=1, keepdims=True) + EPS)


def pick_kernel(odd_takes, image, text, unit, raw, sem):
    rows = raw.shape[0] // CHUNKS
    takes_image = lax.rem(lax.axis_index("blk"), 2) != odd_takes

    def copy(source, c):
        part = pl.ds(c * rows, rows)
        return pltpu.make_async_copy(source.at[part], raw.at[part], sem.at[c])

    @pl.when(takes_image)
    def _():
        for c in range(CHUNKS):
            copy(image, c).start()

    @pl.when(jnp.logical_not(takes_image))
    def _():
        for c in range(CHUNKS):
            copy(text, c).start()

    extra = unit.shape[0] - raw.shape[0]
    if extra:
        unit[raw.shape[0] :] = jnp.zeros((extra, raw.shape[1]), F32)
    for c in range(CHUNKS):
        copy(image, c).wait()
        part = pl.ds(c * rows, rows)
        value = raw[part]
        unit[part] = value * inverse_norm(value)


def split_kernel(value, high, low, raw, sem):
    read = pltpu.make_async_copy(value, raw, sem)
    read.start()
    read.wait()
    high[...], low[...] = split(raw[...])


def middle_kernel(scale, shift, yh, yl, y1s, sent, tile, sh, sl):
    rows, width = yh.shape

    @step(0)
    def _():
        sh[...], sl[...] = split(y1s[...])
        tile[...] = logits((yh[...], yl[...]), (sh[...], sl[...]))

    @step(1)
    def _():
        terms, weight = pair_terms(tile[...], scale[0], shift[0])
        sent[:rows] = spread(weight, (sh[...], sl[...]))
        sent[rows:, :rows] = row_sums(terms)
        sent[rows:, rows:] = jnp.zeros((8, width - rows), F32)


def own_kernel(scale, shift, p, q, grad_p, grad_q, loss_p, loss_q, ph, plo, qh, qlo, tile):
    rows = ph.shape[0]

    @step(0)
    def _():
        ph[...], plo[...] = split(p[...])
        qh[...], qlo[...] = split(q[:rows])
        tile[...] = logits((ph[...], plo[...]), (qh[...], qlo[...]))

    @step(1)
    def _():
        terms, weight = pair_terms(tile[...], scale[0], shift[0], own=True)
        loss_p[...] = terms
        loss_q[...] = jnp.transpose(terms)
        grad_p[...] = spread(weight, (qh[...], qlo[...]))
        grad_q[...] = spread(jnp.transpose(weight), (ph[...], plo[...]))


def add_first(
    scale, shift, ph, plo, qh, qlo, yh, yl, y1s, z, gp_in, gq_in, lp_in, lq_in, grad_p, grad_q, loss_p, loss_q, scratch
):
    sh, sl, zh, zl, tile_y, tile_s, tile_z, z_raw, sem = scratch
    rows = ph.shape[0]
    read = pltpu.make_async_copy(z.at[pl.ds(0, rows)], z_raw, sem)

    def logit_part():
        read.start()
        tile_y[...] = logits((ph[...], plo[...]), (yh[...], yl[...]))
        sh[...], sl[...] = split(y1s[...])
        tile_s[...] = logits((qh[...], qlo[...]), (sh[...], sl[...]))

    def partner_part():
        read.wait()
        zh[...], zl[...] = split(z_raw[...])
        tile_z[...] = logits((qh[...], qlo[...]), (zh[...], zl[...]))

    def gradient_part():
        terms_y, weight_y = pair_terms(tile_y[...], scale[0], shift[0])
        terms_s, weight_s = pair_terms(tile_s[...], scale[0], shift[0])
        terms_z, weight_z = pair_terms(tile_z[...], scale[0], shift[0])
        loss_p[...] = lp_in[...] + terms_y
        loss_q[...] = lq_in[...] + terms_s + terms_z
        grad_p[...] = gp_in[...] + spread(weight_y, (yh[...], yl[...]))
        grad_q[...] = gq_in[...] + spread(weight_s, (sh[...], sl[...])) + spread(weight_z, (zh[...], zl[...]))

    return logit_part, partner_part, gradient_part


def odd_first_kernel(
    scale, shift, ph, plo, qh, qlo, yh, yl, y1s, z, gp_in, gq_in, lp_in, lq_in, after, grad_p, grad_q, loss_p, loss_q, *scratch
):
    parts = add_first(
        scale, shift, ph, plo, qh, qlo, yh, yl, y1s, z, gp_in, gq_in, lp_in, lq_in, grad_p, grad_q, loss_p, loss_q, scratch
    )
    for part in parts:
        pl.when(lax.rem(lax.axis_index("blk"), 2) == 1)(part)


def even_first_kernel(
    scale, shift, ph, plo, qh, qlo, yh, yl, y1s, z, y2, image, text, gp_in, gq_in, lp_in, lq_in,
    grad_p, grad_q, loss_p, loss_q, inv_p, inv_q, wh, wl, tile_w, raw, raw_sem, *scratch
):
    reads = [pltpu.make_async_copy(side, raw.at[i], raw_sem.at[i]) for i, side in enumerate((image, text))]
    for read in reads:
        read.start()
    parts = add_first(
        scale, shift, ph, plo, qh, qlo, yh, yl, y1s, z, gp_in, gq_in, lp_in, lq_in, grad_p, grad_q, loss_p, loss_q, scratch
    )
    for part in parts:
        pl.when(lax.rem(lax.axis_index("blk"), 2) == 0)(part)

    @step(0)
    def _():
        wh[...], wl[...] = split(y2[: wh.shape[0]])
        tile_w[...] = logits((ph[...], plo[...]), (wh[...], wl[...]))

    @step(1)
    def _():
        terms, weight = pair_terms(tile_w[...], scale[0], shift[0])
        loss_p[...] = lp_in[...] + terms
        grad_p[...] = gp_in[...] + spread(weight, (wh[...], wl[...]))

    for read in reads:
        read.wait()
    odd = lax.rem(lax.axis_index("blk"), 2)
    inv_p[...] = jnp.broadcast_to(inverse_norm(raw[odd]), inv_p.shape)
    inv_q[...] = jnp.broadcast_to(inverse_norm(raw[1 - odd]), inv_q.shape)


def restored(unit, inverse, grad):
    inner = jnp.sum(unit * grad, axis=1, keepdims=True)
    return inverse * (grad - inner * unit)


def put(value_ref, image_out, text_out, to_image, sem, c, rows):
    part = pl.ds(c * rows, rows)

    @pl.when(to_image)
    def _():
        pltpu.make_async_copy(value_ref.at[part], image_out.at[part], sem.at[c]).start()

    @pl.when(jnp.logical_not(to_image))
    def _():
        pltpu.make_async_copy(value_ref.at[part], text_out.at[part], sem.at[c]).start()


def finish(unit, inverse, grad, image_out, text_out, result, sem, to_image):
    rows = result.shape[0] // CHUNKS
    for c in range(CHUNKS):
        part = pl.ds(c * rows, rows)
        result[part] = restored(unit[part], inverse[part][:, :1], grad(part))
        put(result, image_out, text_out, to_image, sem, c, rows)
    for c in range(CHUNKS):
        part = pl.ds(c * rows, rows)
        pltpu.make_async_copy(result.at[part], image_out.at[part], sem.at[c]).wait()


def second_kernel(
    scale, shift, qh, qlo, y2s, gq_in, lq_in, lp_in, q, inv_q,
    image_out, text_out, loss_q, loss_p, sh, sl, tile_s, result, sem
):
    @step(0)
    def _():
        sh[...], sl[...] = split(y2s[...])
        tile_s[...] = logits((qh[...], qlo[...]), (sh[...], sl[...]))

    odd = lax.rem(lax.axis_index("blk"), 2) == 1
    rows = result.shape[0] // 2
    for h in range(2):
        part = pl.ds(h * rows, rows)

        @step(1 + h)
        def _():
            terms, weight = pair_terms(tile_s[part], scale[0], shift[0])
            grad = gq_in[part] + spread(weight, (sh[...], sl[...]))
            result[part] = restored(q[part], inv_q[part][:, :1], grad)
            tile_s[part] = lq_in[part] + terms
            put(result, image_out, text_out, odd, sem, h, rows)

    loss_q[...] = row_sums(tile_s[...])
    loss_p[...] = row_sums(lp_in[...])
    for h in range(2):
        part = pl.ds(h * rows, rows)
        pltpu.make_async_copy(result.at[part], image_out.at[part], sem.at[h]).wait()


def last_kernel(
    gp_in, returned, p, inv_p, loss_p, loss_q, image_in, text_in, loss, image_out, text_out, result, sem, line, line_sem
):
    rows = result.shape[0]
    even = lax.rem(lax.axis_index("blk"), 2) == 0
    total = jnp.where(even, loss_p[:1] + returned[rows : rows + 1, :rows], loss_q[:1])
    line[...] = total * (1.0 / HOPS)
    copy = pltpu.make_async_copy(line, loss, line_sem)
    copy.start()
    finish(
        p, inv_p, lambda part: gp_in[part] + returned[part], image_out, text_out, result, sem, even
    )
    copy.wait()


def call(kernel, ins, outs, scratch=(), aliases=None, cost=0):
    arrays, specs = [], []
    for array, place in ins:
        specs.append(pl.BlockSpec(memory_space=place))
        arrays.append(pltpu.with_memory_space_constraint(array, place) if place in (pltpu.VMEM, pltpu.HBM) else array)
    return pl.pallas_call(
        kernel,
        out_shape=[o for o, _ in outs],
        in_specs=specs,
        out_specs=[pl.BlockSpec(memory_space=place) for _, place in outs],
        scratch_shapes=list(scratch),
        input_output_aliases=aliases or {},
        compiler_params=pltpu.CompilerParams(vmem_limit_bytes=VMEM_LIMIT),
        cost_estimate=pl.CostEstimate(flops=0, transcendentals=0, bytes_accessed=cost),
    )(*arrays)


def body(picture_vectors, caption_vectors, sharpness_factor, additive_shift_term):
    rows, width = picture_vectors.shape
    block = (rows, width)
    vm, hbm, sm, anywhere = pltpu.VMEM, pltpu.HBM, pltpu.SMEM, pl.ANY

    def fast(shape=block, dtype=F32):
        return (pltpu.VMEM(shape, dtype), vm)

    scalars = [(sharpness_factor, sm), (additive_shift_term, sm)]

    def v(*arrays):
        return [(a, vm) for a in arrays]

    def pick(odd_takes, taken, cost):
        return call(
            functools.partial(pick_kernel, odd_takes),
            [(picture_vectors, hbm), (caption_vectors, hbm)],
            [fast((taken, width))],
            [pltpu.VMEM(block, F32), pltpu.SemaphoreType.DMA((CHUNKS,))],
            cost=cost,
        )

    line, square, half = (8, rows), (rows, rows), pltpu.VMEM(block, BF16)
    tile = pltpu.VMEM(square, F32)
    (p,) = pick(1, rows, 0)
    y1 = across(p)
    (q,) = pick(0, rows + PAD, COST_Q)
    z = lax.cond(lax.axis_index("blk") < 1 << 20, in_chip, in_chip_in_halves, q)
    y2 = across(z)
    grad_p, grad_q, loss_p, loss_q, ph, plo, qh, qlo = call(
        own_kernel,
        scalars + v(p, q),
        [fast(), fast(), fast(square), fast(square)] + [fast(block, BF16)] * 4,
        [tile],
        cost=COST_OWN,
    )
    y1, grad_p = lax.optimization_barrier((y1, grad_p))
    y1s = in_chip(y1)
    yh, yl = call(
        split_kernel,
        [(y1, hbm)],
        [fast(block, BF16)] * 2,
        [pltpu.VMEM(block, F32), pltpu.SemaphoreType.DMA],
        cost=COST_SPLIT,
    )
    (sent,) = call(
        middle_kernel,
        scalars + v(yh, yl, y1s),
        [fast((rows + 8, width))],
        [tile] + [half] * 2,
    )
    returned = across(sent)
    state = [grad_p, grad_q, loss_p, loss_q]
    outs = [fast(), fast(), fast(square), fast(square)]
    scratch = [half] * 4 + [tile] * 3 + [pltpu.VMEM(block, F32), pltpu.SemaphoreType.DMA]
    state = call(
        odd_first_kernel,
        scalars + v(ph, plo, qh, qlo, yh, yl, y1s) + [(z, hbm)] + v(*state) + [(sent, anywhere)],
        outs,
        scratch,
        {10 + i: i for i in range(4)},
    )
    y2, state = lax.optimization_barrier((y2, state))
    y2s = in_chip(y2[:rows])
    grad_p, grad_q, loss_p, loss_q, inv_p, inv_q = call(
        even_first_kernel,
        scalars + v(ph, plo, qh, qlo, yh, yl, y1s) + [(z, hbm)] + v(y2) + [(picture_vectors, hbm), (caption_vectors, hbm)] + v(*state),
        outs + [fast((rows, 128))] * 2,
        [half, half, tile, pltpu.VMEM((2, rows, width), F32), pltpu.SemaphoreType.DMA((2,))] + scratch,
        {13 + i: i for i in range(4)},
    )
    whole = (jax.ShapeDtypeStruct(block, F32), hbm)
    out_scratch = [pltpu.VMEM(block, F32), pltpu.SemaphoreType.DMA((CHUNKS,))]
    image_out, text_out, loss_q, loss_p = call(
        second_kernel,
        scalars + v(qh, qlo, y2s, grad_q, loss_q, loss_p, q, inv_q),
        [whole, whole, fast(line), fast(line)],
        [half] * 2 + [tile] + out_scratch,
    )
    loss, grad_image, text_gradient = call(
        last_kernel,
        v(grad_p, returned, p, inv_p, loss_p, loss_q) + [(image_out, hbm), (text_out, hbm)],
        [(jax.ShapeDtypeStruct((1, rows), F32), hbm), whole, whole],
        out_scratch + [pltpu.VMEM((1, rows), F32), pltpu.SemaphoreType.DMA],
        {6: 1, 7: 2},
    )
    return (loss.reshape(rows), grad_image, text_gradient)


def solution(mesh):
    placed = (P("blk", None), P("blk", None), P(), P())
    return jax.shard_map(
        body,
        mesh=mesh,
        in_specs=placed,
        out_specs=(P("blk"), P("blk", None), P("blk", None)),
        check_vma=False,
    )
```

```python
import functools

import jax
import jax.numpy as jnp
from jax import lax
from jax.experimental import pallas as pl
from jax.experimental.pallas import tpu as pltpu
from jax.sharding import PartitionSpec as P

HOPS = 4
EPS = 1e-06
F32 = jnp.float32
BF16 = jnp.bfloat16
READ_ROWS = (64, 64, 64, 64)
WRITE_ROWS = (16, 64, 80, 96)
PAD = 8
COST_Q = 8000000
COST_OWN = 8000000
COST_SPLIT = 4000000
VMEM_LIMIT = 20 * 1024 * 1024


def across(value):
    count = lax.axis_size("blk")
    pairs = [(i, (i + 1 if i % 2 else i - 1) % count) for i in range(count)]
    return lax.ppermute(value, "blk", pairs)


def in_chip(value):
    count = lax.axis_size("blk")
    return lax.ppermute(value, "blk", [(i, i ^ 1) for i in range(count)])


def in_chip_in_halves(value):
    half = value.shape[0] // 2
    return jnp.concatenate([in_chip(value[:half]), in_chip(value[half:])], axis=0)


def split(value):
    high = value.astype(BF16)
    return high, (value - high.astype(F32)).astype(BF16)


def product(a, b, contract):
    def one(x, y):
        return lax.dot_general(x, y, (contract, ((), ())), preferred_element_type=F32)

    return one(a[0], b[0]) + (one(a[0], b[1]) + one(a[1], b[0]))


def logits(rows, others):
    return product(rows, others, ((1,), (1,)))


def pair_terms(logit, scale, shift, own=False):
    shifted = scale * logit + shift
    decay = jnp.exp(-jnp.abs(shifted))
    part = 1.0 / (1.0 + decay)
    sigmoid = jnp.where(shifted >= 0.0, part, decay * part)
    signed = shifted
    if own:
        shape = shifted.shape
        positive = lax.broadcasted_iota(jnp.int32, shape, 0) == lax.broadcasted_iota(jnp.int32, shape, 1)
        signed = jnp.where(positive, -shifted, shifted)
        sigmoid = sigmoid - jnp.where(positive, 1.0, 0.0)
    return jnp.maximum(signed, 0.0) + jnp.log1p(decay), scale * sigmoid


def spread(weight, others):
    return product(split(weight), others, ((1,), (0,)))


def step(number):
    return pl.when(lax.axis_index("blk") < (1 << 20) + number)


def row_sums(terms):
    sums = jnp.sum(terms, axis=1, keepdims=True)
    return jnp.transpose(jnp.broadcast_to(sums, (terms.shape[0], 128)))[:8]


def inverse_norm(value):
    return lax.rsqrt(jnp.sum(value * value, axis=1, keepdims=True) + EPS)


def parts_of(rows):
    starts = [sum(rows[:i]) for i in range(len(rows))]
    return [pl.ds(start, size) for start, size in zip(starts, rows)]


def pick_kernel(odd_takes, image, text, unit, raw, sem):
    parts = parts_of(READ_ROWS)
    takes_image = lax.rem(lax.axis_index("blk"), 2) != odd_takes

    def copy(source, c):
        part = parts[c]
        return pltpu.make_async_copy(source.at[part], raw.at[part], sem.at[c])

    @pl.when(takes_image)
    def _():
        for c in range(len(parts)):
            copy(image, c).start()

    @pl.when(jnp.logical_not(takes_image))
    def _():
        for c in range(len(parts)):
            copy(text, c).start()

    extra = unit.shape[0] - raw.shape[0]
    if extra:
        unit[raw.shape[0] :] = jnp.zeros((extra, raw.shape[1]), F32)
    for c in range(len(parts)):
        copy(image, c).wait()
        part = parts[c]
        value = raw[part]
        unit[part] = value * inverse_norm(value)


def split_kernel(value, high, low, raw, sem):
    read = pltpu.make_async_copy(value, raw, sem)
    read.start()
    read.wait()
    high[...], low[...] = split(raw[...])


def middle_kernel(scale, shift, yh, yl, y1s, sent, tile, sh, sl):
    rows, width = yh.shape

    @step(0)
    def _():
        sh[...], sl[...] = split(y1s[...])
        tile[...] = logits((yh[...], yl[...]), (sh[...], sl[...]))

    @step(1)
    def _():
        terms, weight = pair_terms(tile[...], scale[0], shift[0])
        sent[:rows] = spread(weight, (sh[...], sl[...]))
        sent[rows:, :rows] = row_sums(terms)
        sent[rows:, rows:] = jnp.zeros((8, width - rows), F32)


def own_kernel(scale, shift, p, q, grad_p, grad_q, loss_p, loss_q, ph, plo, qh, qlo, tile):
    rows = ph.shape[0]

    @step(0)
    def _():
        ph[...], plo[...] = split(p[...])
        qh[...], qlo[...] = split(q[:rows])
        tile[...] = logits((ph[...], plo[...]), (qh[...], qlo[...]))

    @step(1)
    def _():
        terms, weight = pair_terms(tile[...], scale[0], shift[0], own=True)
        loss_p[...] = terms
        loss_q[...] = jnp.transpose(terms)
        grad_p[...] = spread(weight, (qh[...], qlo[...]))
        grad_q[...] = spread(jnp.transpose(weight), (ph[...], plo[...]))


def add_first(
    scale, shift, ph, plo, qh, qlo, yh, yl, y1s, z, gp_in, gq_in, lp_in, lq_in, grad_p, grad_q, loss_p, loss_q, scratch
):
    sh, sl, zh, zl, tile_y, tile_s, tile_z, z_raw, sem = scratch
    rows = ph.shape[0]
    read = pltpu.make_async_copy(z.at[pl.ds(0, rows)], z_raw, sem)

    def logit_part():
        read.start()
        tile_y[...] = logits((ph[...], plo[...]), (yh[...], yl[...]))
        sh[...], sl[...] = split(y1s[...])
        tile_s[...] = logits((qh[...], qlo[...]), (sh[...], sl[...]))

    def partner_part():
        read.wait()
        zh[...], zl[...] = split(z_raw[...])
        tile_z[...] = logits((qh[...], qlo[...]), (zh[...], zl[...]))

    def gradient_part():
        terms_y, weight_y = pair_terms(tile_y[...], scale[0], shift[0])
        terms_s, weight_s = pair_terms(tile_s[...], scale[0], shift[0])
        terms_z, weight_z = pair_terms(tile_z[...], scale[0], shift[0])
        loss_p[...] = lp_in[...] + terms_y
        loss_q[...] = lq_in[...] + terms_s + terms_z
        grad_p[...] = gp_in[...] + spread(weight_y, (yh[...], yl[...]))
        grad_q[...] = gq_in[...] + spread(weight_s, (sh[...], sl[...])) + spread(weight_z, (zh[...], zl[...]))

    return logit_part, partner_part, gradient_part


def odd_first_kernel(
    scale, shift, ph, plo, qh, qlo, yh, yl, y1s, z, gp_in, gq_in, lp_in, lq_in, after, grad_p, grad_q, loss_p, loss_q, *scratch
):
    parts = add_first(
        scale, shift, ph, plo, qh, qlo, yh, yl, y1s, z, gp_in, gq_in, lp_in, lq_in, grad_p, grad_q, loss_p, loss_q, scratch
    )
    for part in parts:
        pl.when(lax.rem(lax.axis_index("blk"), 2) == 1)(part)


def even_first_kernel(
    scale, shift, ph, plo, qh, qlo, yh, yl, y1s, z, y2, image, text, gp_in, gq_in, lp_in, lq_in,
    grad_p, grad_q, loss_p, loss_q, inv_p, inv_q, wh, wl, tile_w, raw, raw_sem, *scratch
):
    reads = [pltpu.make_async_copy(side, raw.at[i], raw_sem.at[i]) for i, side in enumerate((image, text))]
    for read in reads:
        read.start()
    parts = add_first(
        scale, shift, ph, plo, qh, qlo, yh, yl, y1s, z, gp_in, gq_in, lp_in, lq_in, grad_p, grad_q, loss_p, loss_q, scratch
    )
    for part in parts:
        pl.when(lax.rem(lax.axis_index("blk"), 2) == 0)(part)

    @step(0)
    def _():
        wh[...], wl[...] = split(y2[: wh.shape[0]])
        tile_w[...] = logits((ph[...], plo[...]), (wh[...], wl[...]))

    @step(1)
    def _():
        terms, weight = pair_terms(tile_w[...], scale[0], shift[0])
        loss_p[...] = lp_in[...] + terms
        grad_p[...] = gp_in[...] + spread(weight, (wh[...], wl[...]))

    for read in reads:
        read.wait()
    odd = lax.rem(lax.axis_index("blk"), 2)
    inv_p[...] = jnp.broadcast_to(inverse_norm(raw[odd]), inv_p.shape)
    inv_q[...] = jnp.broadcast_to(inverse_norm(raw[1 - odd]), inv_q.shape)


def restored(unit, inverse, grad):
    inner = jnp.sum(unit * grad, axis=1, keepdims=True)
    return inverse * (grad - inner * unit)


def put(value_ref, image_out, text_out, to_image, sem, c, part):
    @pl.when(to_image)
    def _():
        pltpu.make_async_copy(value_ref.at[part], image_out.at[part], sem.at[c]).start()

    @pl.when(jnp.logical_not(to_image))
    def _():
        pltpu.make_async_copy(value_ref.at[part], text_out.at[part], sem.at[c]).start()


def finish(unit, inverse, grad, image_out, text_out, result, sem, to_image):
    parts = parts_of(WRITE_ROWS)
    for c, part in enumerate(parts):
        result[part] = restored(unit[part], inverse[part][:, :1], grad(part))
        put(result, image_out, text_out, to_image, sem, c, part)
    for c, part in enumerate(parts):
        pltpu.make_async_copy(result.at[part], image_out.at[part], sem.at[c]).wait()


def second_kernel(
    scale, shift, qh, qlo, y2s, gq_in, lq_in, lp_in, q, inv_q,
    image_out, text_out, loss_q, loss_p, sh, sl, tile_s, result, sem
):
    @step(0)
    def _():
        sh[...], sl[...] = split(y2s[...])
        tile_s[...] = logits((qh[...], qlo[...]), (sh[...], sl[...]))

    odd = lax.rem(lax.axis_index("blk"), 2) == 1
    rows = result.shape[0] // 2
    for h in range(2):
        part = pl.ds(h * rows, rows)

        @step(1 + h)
        def _():
            terms, weight = pair_terms(tile_s[part], scale[0], shift[0])
            grad = gq_in[part] + spread(weight, (sh[...], sl[...]))
            result[part] = restored(q[part], inv_q[part][:, :1], grad)
            tile_s[part] = lq_in[part] + terms
            put(result, image_out, text_out, odd, sem, h, part)

    loss_q[...] = row_sums(tile_s[...])
    loss_p[...] = row_sums(lp_in[...])
    for h in range(2):
        part = pl.ds(h * rows, rows)
        pltpu.make_async_copy(result.at[part], image_out.at[part], sem.at[h]).wait()


def last_kernel(
    gp_in, returned, p, inv_p, loss_p, loss_q, image_in, text_in, loss, image_out, text_out, result, sem, line, line_sem
):
    rows = result.shape[0]
    even = lax.rem(lax.axis_index("blk"), 2) == 0
    total = jnp.where(even, loss_p[:1] + returned[rows : rows + 1, :rows], loss_q[:1])
    line[...] = total * (1.0 / HOPS)
    copy = pltpu.make_async_copy(line, loss, line_sem)
    copy.start()
    finish(
        p, inv_p, lambda part: gp_in[part] + returned[part], image_out, text_out, result, sem, even
    )
    copy.wait()


def call(kernel, ins, outs, scratch=(), aliases=None, cost=0):
    arrays, specs = [], []
    for array, place in ins:
        specs.append(pl.BlockSpec(memory_space=place))
        arrays.append(pltpu.with_memory_space_constraint(array, place) if place in (pltpu.VMEM, pltpu.HBM) else array)
    return pl.pallas_call(
        kernel,
        out_shape=[o for o, _ in outs],
        in_specs=specs,
        out_specs=[pl.BlockSpec(memory_space=place) for _, place in outs],
        scratch_shapes=list(scratch),
        input_output_aliases=aliases or {},
        compiler_params=pltpu.CompilerParams(vmem_limit_bytes=VMEM_LIMIT),
        cost_estimate=pl.CostEstimate(flops=0, transcendentals=0, bytes_accessed=cost),
    )(*arrays)


def body(picture_vectors, caption_vectors, sharpness_factor, additive_shift_term):
    rows, width = picture_vectors.shape
    block = (rows, width)
    vm, hbm, sm, anywhere = pltpu.VMEM, pltpu.HBM, pltpu.SMEM, pl.ANY

    def fast(shape=block, dtype=F32):
        return (pltpu.VMEM(shape, dtype), vm)

    scalars = [(sharpness_factor, sm), (additive_shift_term, sm)]

    def v(*arrays):
        return [(a, vm) for a in arrays]

    def pick(odd_takes, taken, cost):
        return call(
            functools.partial(pick_kernel, odd_takes),
            [(picture_vectors, hbm), (caption_vectors, hbm)],
            [fast((taken, width))],
            [pltpu.VMEM(block, F32), pltpu.SemaphoreType.DMA((4,))],
            cost=cost,
        )

    line, square, half = (8, rows), (rows, rows), pltpu.VMEM(block, BF16)
    tile = pltpu.VMEM(square, F32)
    (p,) = pick(1, rows, 0)
    y1 = across(p)
    (q,) = pick(0, rows + PAD, COST_Q)
    z = lax.cond(lax.axis_index("blk") < 1 << 20, in_chip, in_chip_in_halves, q)
    y2 = across(z)
    grad_p, grad_q, loss_p, loss_q, ph, plo, qh, qlo = call(
        own_kernel,
        scalars + v(p, q),
        [fast(), fast(), fast(square), fast(square)] + [fast(block, BF16)] * 4,
        [tile],
        cost=COST_OWN,
    )
    y1, grad_p = lax.optimization_barrier((y1, grad_p))
    y1s = in_chip(y1)
    yh, yl = call(
        split_kernel,
        [(y1, hbm)],
        [fast(block, BF16)] * 2,
        [pltpu.VMEM(block, F32), pltpu.SemaphoreType.DMA],
        cost=COST_SPLIT,
    )
    (sent,) = call(
        middle_kernel,
        scalars + v(yh, yl, y1s),
        [fast((rows + 8, width))],
        [tile] + [half] * 2,
    )
    returned = across(sent)
    state = [grad_p, grad_q, loss_p, loss_q]
    outs = [fast(), fast(), fast(square), fast(square)]
    scratch = [half] * 4 + [tile] * 3 + [pltpu.VMEM(block, F32), pltpu.SemaphoreType.DMA]
    state = call(
        odd_first_kernel,
        scalars + v(ph, plo, qh, qlo, yh, yl, y1s) + [(z, hbm)] + v(*state) + [(sent, anywhere)],
        outs,
        scratch,
        {10 + i: i for i in range(4)},
    )
    y2, state = lax.optimization_barrier((y2, state))
    y2s = in_chip(y2[:rows])
    grad_p, grad_q, loss_p, loss_q, inv_p, inv_q = call(
        even_first_kernel,
        scalars + v(ph, plo, qh, qlo, yh, yl, y1s) + [(z, hbm)] + v(y2) + [(picture_vectors, hbm), (caption_vectors, hbm)] + v(*state),
        outs + [fast((rows, 128))] * 2,
        [half, half, tile, pltpu.VMEM((2, rows, width), F32), pltpu.SemaphoreType.DMA((2,))] + scratch,
        {13 + i: i for i in range(4)},
    )
    whole = (jax.ShapeDtypeStruct(block, F32), hbm)
    out_scratch = [pltpu.VMEM(block, F32), pltpu.SemaphoreType.DMA((4,))]
    image_out, text_out, loss_q, loss_p = call(
        second_kernel,
        scalars + v(qh, qlo, y2s, grad_q, loss_q, loss_p, q, inv_q),
        [whole, whole, fast(line), fast(line)],
        [half] * 2 + [tile] + out_scratch,
    )
    loss, grad_image, text_gradient = call(
        last_kernel,
        v(grad_p, returned, p, inv_p, loss_p, loss_q) + [(image_out, hbm), (text_out, hbm)],
        [(jax.ShapeDtypeStruct((1, rows), F32), hbm), whole, whole],
        out_scratch + [pltpu.VMEM((1, rows), F32), pltpu.SemaphoreType.DMA],
        {6: 1, 7: 2},
    )
    return (loss.reshape(rows), grad_image, text_gradient)


def solution(mesh):
    placed = (P("blk", None), P("blk", None), P(), P())
    return jax.shard_map(
        body,
        mesh=mesh,
        in_specs=placed,
        out_specs=(P("blk"), P("blk", None), P("blk", None)),
        check_vma=False,
    )
```
